128 devices in a mesh: wide: 16 (over x, z), narrow: 8 (over y, core).
Axes of the slice: x: 4, y: 4, z: 4, core: 2. Of those that a mesh axis runs over, the one named last changes fastest.
Arguments:
- pair_density: bfloat16 [2, 7680, 6144], P(None, ('wide', 'narrow')), may hold values from -0.21875 to 0.21875
- g_index: int32 [7680], P(('wide', 'narrow')), may hold values from 0 to 15359, as said below
- coulomb_table: float32 [15360], replicated, may hold values from 0.1 to 10
- eps_valence: float32 [300], replicated, may hold values from -20 to -4
- eps_conduction: float32 [300], replicated, may hold values from 4 to 20
- valence_band: int32 [6144], P('narrow'), may hold values from 0 to 299
- conduction_band: int32 [6144], P('narrow'), may hold values from 0 to 299
Outputs:
- hamiltonian: float32 [2, 6144, 6144], P(None, 'narrow', 'wide')
The draws below stay inside these ranges and needn't reach their ends.
Inputs may be any that keep to these rules, and one draw needn't show every extreme that they name: `g_index`: increasing; entry i is 2 i or 2 i + 1, so all entries differ.
All inputs are finite; a program needn't handle non-finite values.
Results may differ from the reference program's by a relative error of at most 0.0045.
Values may be sent and summed in bfloat16 or wider, within the bound.
No kernel may reach another device: no remote copies, remote signals or barrier semaphores. Data moves between devices by JAX's collectives and lax.ppermute only.
A program may use at most 320 MiB of HBM per device.

```python
import math
import jax
import jax.numpy as jnp

NG = 7680
NV = 300
NC = 300
NT = 6144
NG_ALL = 15360


def draw_g_index(key, part):
    key = jax.random.fold_in(key, 7)
    offset_bits = jax.random.randint(key, (NG,), 0, 2)
    position = jnp.arange(NG)
    offset_bits = jnp.where(position == 0, 0, jnp.where(position == NG - 1, 1, offset_bits))
    return (2 * position + offset_bits).astype(jnp.int32)


def touch_ends(drawn, rng, low, high):
    longest = drawn.shape.index(max(drawn.shape))
    spots = []
    for shift in (0, 1):
        where = [jax.random.randint(jax.random.fold_in(rng, axis), (), 0, length) for axis, length in enumerate(drawn.shape)]
        where[longest] = (where[longest] + shift) % drawn.shape[longest]
        spots.append(tuple(where))
    return drawn.at[spots[0]].set(low).at[spots[1]].set(high)


def level_of(stream_key, dims, shards, smallest, top_value):
    def one(dim, blocks):
        steps = jax.random.uniform(jax.random.fold_in(jax.random.fold_in(stream_key, 6), dim), (blocks,), jnp.float32, smallest / len(shards), top_value / len(shards))
        return jnp.repeat(jnp.exp(steps), dims[dim] // blocks).reshape((-1,) + (1,) * (len(dims) - dim - 1))

    level = one(*shards[0])
    for cut in shards[1:]:
        level = level * one(*cut)
    return level


def normal_values(rng, shape, width, reach, pieces=(), held_as=jnp.bfloat16):
    result = jax.random.normal(rng, shape, jnp.float32) * width
    if len(pieces) > 0:
        result = level_of(rng, shape, pieces, -0.22, 0.18) * result
    return jnp.clip(result, min=-reach, max=reach).astype(held_as)


def setup_inputs(seed: int = 0) -> dict:
    streams_of = jax.random.split(jax.random.key(seed), 8)
    return {
        "pair_density": normal_values(streams_of[0], (2, NG, NT), 0.035, 0.21875, ((1, 128),)),
        "g_index": draw_g_index(jax.random.fold_in(streams_of[7], 71), 0),
        "coulomb_table": jnp.clip(jnp.exp(jax.random.uniform(streams_of[2], (NG_ALL,), jnp.float32, math.log(0.1), math.log(10.0))), 0.1, 10.0),
        "eps_valence": jnp.clip(jax.random.uniform(streams_of[3], (NV,), jnp.float32, -20.0, -4.0), -20.0, -4.0),
        "eps_conduction": jnp.clip(jax.random.uniform(streams_of[4], (NC,), jnp.float32, 4.0, 20.0), 4.0, 20.0),
        "valence_band": touch_ends(jax.random.randint(streams_of[5], (NT,), 0, NV), jax.random.fold_in(streams_of[5], 1), 0, NV - 1).astype(jnp.int32),
        "conduction_band": touch_ends(jax.random.randint(streams_of[6], (NT,), 0, NC), jax.random.fold_in(streams_of[6], 1), 0, NC - 1).astype(jnp.int32),
    }


def reference(pair_density, g_index, coulomb_table, eps_valence, eps_conduction, valence_band, conduction_band):
    weight = jnp.sqrt(coulomb_table[g_index])
    scaled = (pair_density.astype(jnp.float32) * weight[None, :, None]).astype(jnp.bfloat16)
    real_first = jnp.dot(scaled[0].T, scaled[0], preferred_element_type=jnp.float32)
    real_second = jnp.dot(scaled[1].T, scaled[1], preferred_element_type=jnp.float32)
    kernel_real = real_first + real_second
    imag_first = jnp.dot(scaled[0].T, scaled[1], preferred_element_type=jnp.float32)
    imag_second = jnp.dot(scaled[1].T, scaled[0], preferred_element_type=jnp.float32)
    kernel_imag = imag_first - imag_second
    energy_gap = eps_conduction[conduction_band] - eps_valence[valence_band]
    real_out = 2.0 * kernel_real + jnp.diag(energy_gap)
    return jnp.stack([real_out, 2.0 * kernel_imag])
```

```python
import functools

import jax
import jax.numpy as jnp
from jax import lax
from jax.experimental import pallas as pl
from jax.experimental.pallas import tpu as pltpu
from jax.sharding import PartitionSpec as P

AXES = ("wide", "narrow")
SIDE = 4
BLOCK = 384
ROW_CHUNKS = ((0, 1),)
COL_CHUNKS = ((2, 1, 3, 0),)


def moved(value, dx=0, dy=0, dz=0, core=0, per_core_z=None):
    pairs = []
    for x in range(SIDE):
        for z in range(SIDE):
            for y in range(SIDE):
                for c in range(2):
                    step = dz if per_core_z is None else per_core_z[c]
                    to = ((x + dx) % SIDE, (z + step) % SIDE, (y + dy) % SIDE, (c + core) % 2)
                    pairs.append(
                        (((x * SIDE + z) * SIDE + y) * 2 + c, ((to[0] * SIDE + to[1]) * SIDE + to[2]) * 2 + to[3])
                    )
    return lax.ppermute(value, AXES, pairs)


def prepare_kernel(pos, own, sib, weight, *outs):
    x, y, z, c = pos[0], pos[1], pos[2], pos[3]
    first = c == 0

    def piece(index):
        cut = pl.ds(pl.multiple_of(index * BLOCK, BLOCK), BLOCK)
        mine = own[:, :, cut].astype(jnp.float32)
        other = sib[:, :, cut].astype(jnp.float32)
        zero = jnp.where(first, mine, other)
        one = jnp.where(first, other, mine)
        rows = jnp.concatenate([zero[0], one[0], zero[1], one[1]], axis=0)
        scale = jnp.concatenate([weight[...]] * (BLOCK // 128), axis=1)
        return (rows * scale).astype(jnp.bfloat16)

    at = 0
    for chunk in ROW_CHUNKS:
        for d in range(SIDE):
            for n, i in enumerate(chunk):
                outs[at][n] = piece((2 * lax.rem(y + d, SIDE) + c) * 2 + i)
            at += 1
    for chunk in COL_CHUNKS:
        for part in range(2):
            for n, delta in enumerate(chunk):
                step = 1 + 2 * c if part == 0 else 2 * c
                outs[at][n] = piece(lax.rem(x + delta, SIDE) * SIDE + lax.rem(z + step, SIDE))
            at += 1


def prepare(pos, own, sib, weight):
    rows = own.shape[1] * 4
    shapes = [
        jax.ShapeDtypeStruct((len(chunk), rows, BLOCK), jnp.bfloat16) for chunk in ROW_CHUNKS for _ in range(SIDE)
    ] + [jax.ShapeDtypeStruct((len(chunk), rows, BLOCK), jnp.bfloat16) for chunk in COL_CHUNKS for _ in range(2)]
    vmem = pl.BlockSpec(memory_space=pltpu.VMEM)
    return pl.pallas_call(
        prepare_kernel,
        out_shape=shapes,
        in_specs=[pl.BlockSpec(memory_space=pltpu.SMEM), vmem, vmem, vmem],
        out_specs=[vmem] * len(shapes),
        compiler_params=pltpu.CompilerParams(vmem_limit_bytes=48 * 2**20),
        cost_estimate=pl.CostEstimate(flops=10**6, bytes_accessed=6 * 10**6, transcendentals=0),
        name="prepare",
    )(pos, own, sib, weight)


def tile_kernel(row_parts, col_parts, row_n, col_at, out_dtype, depth, pos, *refs):
    n_row, n_col = len(row_parts), len(col_parts)
    row_refs, col_refs = refs[:n_row], refs[n_row : n_row + n_col]
    out, rbuf, cbuf, sem = refs[n_row + n_col :]
    c = pos[3]
    copies = []
    for ref, places in zip(row_refs, row_parts):
        for index, zpos, ypos in places:
            zat = jnp.where(c == 0, zpos, SIDE - 1 - zpos)
            start = pl.multiple_of((zat * SIDE + ypos) * depth, depth)
            for i in range(row_n):
                copies.append(
                    pltpu.make_async_copy(
                        ref.at[index, i], rbuf.at[pl.ds(start, depth), pl.ds(i * BLOCK, BLOCK)], sem.at[0]
                    )
                )
    for ref, places in zip(col_refs, col_parts):
        for index, zpos, ypos in places:
            start = (zpos * SIDE + ypos) * depth
            copies.append(
                pltpu.make_async_copy(
                    ref.at[index, col_at], cbuf.at[pl.ds(start, depth), pl.ds(0, BLOCK)], sem.at[0]
                )
            )
    for copy in copies:
        copy.start()
    for copy in copies:
        copy.wait()

    def swap(k, carry):
        at = pl.ds(pl.multiple_of(k * depth, depth), depth)
        value = cbuf[at, :BLOCK].astype(jnp.float32)
        turned = jnp.concatenate([value[depth // 2 :], -value[: depth // 2]], axis=0)
        cbuf[at, BLOCK:] = turned.astype(jnp.bfloat16)
        return carry

    lax.fori_loop(0, SIDE * SIDE, swap, 0)
    total = SIDE * SIDE * depth
    for i in range(row_n):
        prod = lax.dot_general(
            rbuf[:, i * BLOCK : (i + 1) * BLOCK],
            cbuf[...],
            (((0,), (0,)), ((), ())),
            preferred_element_type=jnp.float32,
        )
        prod = 2.0 * prod
        out[0, i * BLOCK : (i + 1) * BLOCK, :] = prod[:, :BLOCK].astype(out_dtype)
        out[1, i * BLOCK : (i + 1) * BLOCK, :] = prod[:, BLOCK:].astype(out_dtype)


def tile(pos, row_ops, col_ops, row_n, col_at, out_dtype):
    depth = row_ops[0][0].shape[-2]
    total = depth * SIDE * SIDE
    kernel = functools.partial(
        tile_kernel, [p for _, p in row_ops], [p for _, p in col_ops], row_n, col_at, out_dtype, depth
    )
    n_in = len(row_ops) + len(col_ops)
    return pl.pallas_call(
        kernel,
        out_shape=jax.ShapeDtypeStruct((2, row_n * BLOCK, BLOCK), out_dtype),
        in_specs=[pl.BlockSpec(memory_space=pltpu.SMEM)] + [pl.BlockSpec(memory_space=pl.ANY)] * n_in,
        out_specs=pl.BlockSpec(memory_space=pltpu.VMEM),
        scratch_shapes=[
            pltpu.VMEM((total, row_n * BLOCK), jnp.bfloat16),
            pltpu.VMEM((total, 2 * BLOCK), jnp.bfloat16),
            pltpu.SemaphoreType.DMA((1,)),
        ],
        compiler_params=pltpu.CompilerParams(vmem_limit_bytes=56 * 2**20),
        cost_estimate=pl.CostEstimate(
            flops=4 * total * row_n * BLOCK * BLOCK, bytes_accessed=2 * total * BLOCK * (row_n + 1), transcendentals=0
        ),
        name="tile",
    )(pos, *[a for a, _ in row_ops], *[a for a, _ in col_ops])


def band_lookup(band_ids, table):
    levels = jnp.arange(table.shape[0], dtype=jnp.int32)
    onehot_mask = band_ids[:, None] == levels[None, :]
    return jnp.sum(jnp.where(onehot_mask, table[None, :], 0.0), axis=1)


def per_device(
    pair_density, g_index, coulomb_table, eps_valence, eps_conduction, valence_band, conduction_band
):
    wide_pos, narrow_pos = lax.axis_index("wide"), lax.axis_index("narrow")
    x, z = wide_pos // SIDE, wide_pos % SIDE
    y, c = narrow_pos // 2, narrow_pos % 2
    pos = jnp.stack([x, y, z, c]).astype(jnp.int32)

    sib = moved(pair_density, core=1)
    sib_index = moved(g_index, core=1)
    chip_index = jnp.where(c == 0, jnp.stack([g_index, sib_index]), jnp.stack([sib_index, g_index]))
    weight = jnp.sqrt(jnp.take(coulomb_table, chip_index.reshape(-1)))
    weight = jnp.broadcast_to(jnp.concatenate([weight, weight])[:, None], (4 * g_index.shape[0], 128))
    pieces = prepare(pos, pair_density, sib, weight)
    row_pieces = [pieces[SIDE * n : SIDE * (n + 1)] for n in range(len(ROW_CHUNKS))]
    rest = pieces[SIDE * len(ROW_CHUNKS) :]
    col_pieces = [rest[2 * n : 2 * (n + 1)] for n in range(len(COL_CHUNKS))]

    row_ops = []
    for group in row_pieces:
        mine = jnp.stack([group[0], moved(group[1], dy=1), moved(group[3], dy=-1), moved(group[2], dy=2)])
        below = moved(mine, dz=1)
        above = moved(mine, dz=-1)
        far_a = moved(below[:2], dz=1)
        far_b = moved(above[2:], dz=-1)
        row_ops.append(
            [
                (mine, [(k, 0, k) for k in range(4)]),
                (below, [(k, 1, k) for k in range(4)]),
                (above, [(k, 2, k) for k in range(4)]),
                (far_a, [(k, 3, k) for k in range(2)]),
                (far_b, [(k, 3, k + 2) for k in range(2)]),
            ]
        )
    col_ops = []
    for part0, part1 in col_pieces:
        mine = jnp.stack([moved(part0, per_core_z=(1, -1)), moved(part1, per_core_z=(0, 2))])
        below = moved(mine, dy=1)
        above = moved(mine, dy=-1)
        far_a = moved(below[:1], dy=1)
        far_b = moved(above[1:], dy=-1)
        held = [
            (mine, [(0, 1, 0), (1, 0, 0)]),
            (below, [(0, 1, 1), (1, 0, 1)]),
            (above, [(0, 1, 2), (1, 0, 2)]),
            (far_a, [(0, 1, 3)]),
            (far_b, [(0, 0, 3)]),
        ]
        other = [(moved(a, core=1), [(k, SIDE - 1 - zp, yp) for k, zp, yp in places]) for a, places in held]
        col_ops.append(held + other)

    sums = []
    for rows, chunk in zip(row_ops, ROW_CHUNKS):
        got = {}
        for cols, deltas in zip(col_ops, COL_CHUNKS):
            for n, delta in enumerate(deltas):
                part = tile(pos, rows, cols, len(chunk), n, jnp.float32 if delta == 0 else jnp.bfloat16)
                got[delta] = part if delta == 0 else moved(part, dx=delta)
        sums.append(sum(got[d].astype(jnp.float32) for d in range(1, SIDE)) + got[0])
    total = jnp.concatenate(sums, axis=1)

    row_width, col_width = total.shape[1], total.shape[2]
    row_ids = narrow_pos * row_width + jnp.arange(row_width, dtype=jnp.int32)
    col_ids = wide_pos * col_width + jnp.arange(col_width, dtype=jnp.int32)
    gap = band_lookup(conduction_band, eps_conduction) - band_lookup(valence_band, eps_valence)
    diagonal = jnp.where(row_ids[:, None] == col_ids[None, :], gap[:, None], 0.0)
    return jnp.stack([total[0] + diagonal, total[1]])


def solution(mesh):
    placed = (
        P(None, ("wide", "narrow"), None),
        P(("wide", "narrow")),
        P(),
        P(),
        P(),
        P("narrow"),
        P("narrow"),
    )
    return jax.shard_map(
        per_device, mesh=mesh, in_specs=placed, out_specs=P(None, "narrow", "wide"), check_vma=False
    )
```

```python
import functools

import jax
import jax.numpy as jnp
from jax import lax
from jax.experimental import pallas as pl
from jax.experimental.pallas import tpu as pltpu
from jax.sharding import PartitionSpec as P

AXES = ("wide", "narrow")
SIDE = 4
BLOCK = 384
HALVES = 2
STEPS = ((2, 0), (1, 3))


def moved(value, name, dx=0, dy=0, dz=0, core=0, per_core_z=None):
    pairs = []
    for x in range(SIDE):
        for z in range(SIDE):
            for y in range(SIDE):
                for c in range(2):
                    step = dz if per_core_z is None else per_core_z[c]
                    to = ((x + dx) % SIDE, (z + step) % SIDE, (y + dy) % SIDE, (c + core) % 2)
                    pairs.append(
                        (((x * SIDE + z) * SIDE + y) * 2 + c, ((to[0] * SIDE + to[1]) * SIDE + to[2]) * 2 + to[3])
                    )
    with jax.named_scope(name):
        return lax.ppermute(value, AXES, pairs)


def after(value, *others):
    return lax.optimization_barrier((value, *others))[0]


def prepare_kernel(pos, own, sib, weight, *outs):
    x, y, z, c = pos[0], pos[1], pos[2], pos[3]
    first = c == 0

    def piece(index):
        cut = pl.ds(pl.multiple_of(index * BLOCK, BLOCK), BLOCK)
        mine = own[:, :, cut].astype(jnp.float32)
        other = sib[:, :, cut].astype(jnp.float32)
        zero = jnp.where(first, mine, other)
        one = jnp.where(first, other, mine)
        rows = jnp.concatenate([zero[0], one[0], zero[1], one[1]], axis=0)
        scale = jnp.concatenate([weight[...]] * (BLOCK // 128), axis=1)
        return (rows * scale).astype(jnp.bfloat16)

    at = 0
    for d in range(SIDE):
        for i in range(HALVES):
            outs[at][i] = piece((2 * lax.rem(y + d, SIDE) + c) * HALVES + i)
        at += 1
    for part in range(2):
        for chunk in (STEPS[0] + STEPS[1],):
            for n, delta in enumerate(chunk):
                step = 1 + 2 * c if part == 0 else 2 * c
                outs[at][n] = piece(lax.rem(x + delta, SIDE) * SIDE + lax.rem(z + step, SIDE))
            at += 1


def prepare(pos, own, sib, weight):
    rows = own.shape[1] * 4
    shapes = [jax.ShapeDtypeStruct((HALVES, rows, BLOCK), jnp.bfloat16)] * SIDE
    shapes += [jax.ShapeDtypeStruct((SIDE, rows, BLOCK), jnp.bfloat16)] * 2
    vmem = pl.BlockSpec(memory_space=pltpu.VMEM)
    return pl.pallas_call(
        prepare_kernel,
        out_shape=shapes,
        in_specs=[pl.BlockSpec(memory_space=pltpu.SMEM), vmem, vmem, vmem],
        out_specs=[vmem] * len(shapes),
        compiler_params=pltpu.CompilerParams(vmem_limit_bytes=20 * 2**20),
        cost_estimate=pl.CostEstimate(flops=10**6, bytes_accessed=6 * 10**6, transcendentals=0),
        name="prepare",
    )(pos, own, sib, weight)


def tile_kernel(plan, pos, *refs):
    row_places, col_places, col_at, depth, n_out, added = plan
    n_row, n_col = len(row_places), len(col_places)
    row_refs, refs = refs[:n_row], refs[n_row:]
    col_refs, refs = refs[:n_col], refs[n_col:]
    if added is not None:
        more, refs = refs[0], refs[1:]
    outs, (rbuf, cbuf, acc) = refs[:n_out], refs[n_out:]
    c = pos[3]

    def take_rows(zwant):
        for ref, places in zip(row_refs, row_places):
            for index, zpos, ypos in places:
                if zpos == zwant:
                    rbuf[ypos * depth : (ypos + 1) * depth] = ref[index]

    for k in range(SIDE):
        pl.when(c == 0)(functools.partial(take_rows, k))
        pl.when(c == 1)(functools.partial(take_rows, SIDE - 1 - k))
        for ref, places in zip(col_refs, col_places):
            for index, zpos, ypos in places:
                if zpos == k:
                    value = ref[index, col_at]
                    at = slice(ypos * depth, (ypos + 1) * depth)
                    cbuf[at, :BLOCK] = value
                    value = value.astype(jnp.float32)
                    turned = jnp.concatenate([value[depth // 2 :], -value[: depth // 2]], axis=0)
                    cbuf[at, BLOCK:] = turned.astype(jnp.bfloat16)
        for m in range(0, rbuf.shape[1], 128):
            part = lax.dot_general(
                rbuf[:, m : m + 128], cbuf[...], (((0,), (0,)), ((), ())), preferred_element_type=jnp.float32
            )
            if k == 0:
                acc[m : m + 128] = part
            elif k < SIDE - 1:
                acc[m : m + 128] += part
            else:
                part = 2.0 * (acc[m : m + 128] + part)
                for p in range(2):
                    value = part[:, p * BLOCK : (p + 1) * BLOCK]
                    if added == p:
                        value = value + more[m : m + 128].astype(jnp.float32)
                    if n_out == 2:
                        outs[p][m : m + 128] = value.astype(outs[p].dtype)
                    else:
                        outs[0][p, m : m + 128] = value.astype(outs[0].dtype)


def tile(pos, row_ops, col_ops, col_at, out_dtype, n_out=1, added=None, more=()):
    depth = row_ops[0][0].shape[-2]
    rows = row_ops[0][0].shape[-1]
    plan = ([p for _, p in row_ops], [p for _, p in col_ops], col_at, depth, n_out, added)
    vmem = pl.BlockSpec(memory_space=pltpu.VMEM)
    group = SIDE * depth
    if n_out == 2:
        shapes = [jax.ShapeDtypeStruct((rows, BLOCK), out_dtype)] * 2
    else:
        shapes = jax.ShapeDtypeStruct((2, rows, BLOCK), out_dtype)
    return pl.pallas_call(
        functools.partial(tile_kernel, plan),
        out_shape=shapes,
        in_specs=[pl.BlockSpec(memory_space=pltpu.SMEM)] + [vmem] * (len(row_ops) + len(col_ops) + len(more)),
        out_specs=[vmem] * 2 if n_out == 2 else vmem,
        scratch_shapes=[
            pltpu.VMEM((group, rows), jnp.bfloat16),
            pltpu.VMEM((group, 2 * BLOCK), jnp.bfloat16),
            pltpu.VMEM((rows, 2 * BLOCK), jnp.float32),
        ],
        compiler_params=pltpu.CompilerParams(vmem_limit_bytes=16 * 2**20),
        cost_estimate=pl.CostEstimate(
            flops=40 * SIDE * group * rows * BLOCK,
            bytes_accessed=2 * SIDE * group * (rows + BLOCK),
            transcendentals=0,
        ),
        name="tile",
    )(pos, *[a for a, _ in row_ops], *[a for a, _ in col_ops], *more)


def finish_kernel(half, pos, own, low, high, gap, *refs):
    out = refs[-1]
    rows = own.shape[1]
    row = lax.broadcasted_iota(jnp.int32, (rows, BLOCK), 0) + ((2 * pos[1] + pos[3]) * HALVES + half) * rows
    col = lax.broadcasted_iota(jnp.int32, (rows, BLOCK), 1) + (pos[0] * SIDE + pos[2]) * BLOCK
    real = own[0] + low[0].astype(jnp.float32) + high[0].astype(jnp.float32)
    out[0] = real + jnp.where(row == col, gap[...], 0.0)
    out[1] = own[1] + low[1].astype(jnp.float32) + high[1].astype(jnp.float32)


def finish(pos, half, own, low, high, gap, before=None):
    rows = own.shape[1]
    whole = lambda shape: pl.BlockSpec(shape, lambda i: (0,) * len(shape))
    planes = whole((2, rows, BLOCK))
    return pl.pallas_call(
        functools.partial(finish_kernel, half),
        grid=(1,),
        out_shape=jax.ShapeDtypeStruct((2, HALVES * rows, BLOCK), jnp.float32),
        in_specs=[pl.BlockSpec(memory_space=pltpu.SMEM), planes, planes, planes, pl.BlockSpec((rows, 1), lambda i: (half, 0))]
        + ([] if before is None else [pl.BlockSpec(memory_space=pl.ANY)]),
        out_specs=pl.BlockSpec((2, rows, BLOCK), lambda i: (0, half, 0)),
        input_output_aliases={} if before is None else {5: 0},
        compiler_params=pltpu.CompilerParams(vmem_limit_bytes=16 * 2**20),
        cost_estimate=pl.CostEstimate(flops=10**6, bytes_accessed=5 * 10**6, transcendentals=0),
        name="finish",
    )(pos, own, low, high, gap[:, None], *(() if before is None else (before,)))


def band_lookup(band_ids, table):
    levels = jnp.arange(table.shape[0], dtype=jnp.int32)
    onehot_mask = band_ids[:, None] == levels[None, :]
    return jnp.sum(jnp.where(onehot_mask, table[None, :], 0.0), axis=1)


def near(mine, name, axis):
    return [moved(mine, name, **{axis: step}) for step in (1, -1)]


def far(pair, name, axis, cut):
    return [moved(pair[0][:cut], name, **{axis: 1}), moved(pair[1][cut:], name, **{axis: -1})]


def swapped(held, places, name):
    return [(held, places), (moved(held, name, core=1), [(k, SIDE - 1 - zp, yp) for k, zp, yp in places])]


def row_places(mine, pair, ends):
    return [
        (mine, [(k, 0, k) for k in range(4)]),
        (pair[0], [(k, 1, k) for k in range(4)]),
        (pair[1], [(k, 2, k) for k in range(4)]),
        (ends[0], [(k, 3, k) for k in range(2)]),
        (ends[1], [(k, 3, k + 2) for k in range(2)]),
    ]


MOST = [(2 * n + k, 1 - k, n) for n in range(3) for k in range(2)]
REST = [(0, 1, 3), (1, 0, 3)]


def together(*groups):
    flat = lax.optimization_barrier(tuple(a for group in groups for a in group))
    result, at = [], 0
    for group in groups:
        result.append(list(flat[at : at + len(group)]))
        at += len(group)
    return result


def per_device(
    pair_density, g_index, coulomb_table, eps_valence, eps_conduction, valence_band, conduction_band
):
    wide_pos, narrow_pos = lax.axis_index("wide"), lax.axis_index("narrow")
    x, z = wide_pos // SIDE, wide_pos % SIDE
    y, c = narrow_pos // 2, narrow_pos % 2
    pos = jnp.stack([x, y, z, c]).astype(jnp.int32)

    sib = moved(pair_density, "swap", core=1)
    sib_index = moved(g_index, "swap_index", core=1)
    chip_index = jnp.where(c == 0, jnp.stack([g_index, sib_index]), jnp.stack([sib_index, g_index]))
    weight = jnp.sqrt(jnp.take(coulomb_table, chip_index.reshape(-1)))
    weight = jnp.broadcast_to(jnp.concatenate([weight, weight])[:, None], (4 * g_index.shape[0], 128))
    pieces = prepare(pos, pair_density, sib, weight)
    mine_r = pieces[:SIDE]
    cols0, cols1 = pieces[SIDE:]

    f1, f3, f2 = (moved(mine_r[k], f"r_y{k}", dy=step) for k, step in ((1, 1), (3, -1), (2, 2)))
    e0 = moved(cols0, "c_z1", per_core_z=(1, -1))
    e1 = moved(cols1, "c_z2", per_core_z=(0, 2))
    (f1, f2, f3), (e0, e1) = together((f1, f2, f3), (e0, e1))
    mine_1, mine_2 = (jnp.stack([a[i] for a in (mine_r[0], f1, f3, f2)]) for i in range(HALVES))
    mine_a, mine_b = (jnp.stack([e0[k], e1[k]]) for k in (slice(0, 2), slice(2, 4)))

    pair_1, pair_a = together(near(mine_1, "r1_near", "dz"), near(mine_a, "ca_near", "dy"))
    most_a = swapped(jnp.concatenate([mine_a, *pair_a]), MOST, "ca_core")
    ends_1, ends_a = together(far(pair_1, "r1_far", "dz", 2), far(pair_a, "ca_far", "dy", 1))
    cols_a = most_a + swapped(jnp.concatenate(ends_a), REST, "ca_core")
    rows_1 = row_places(mine_1, pair_1, ends_1)
    mine_2, mine_b = (after(a, *ends_1, *ends_a) for a in (mine_2, mine_b))
    pair_2, pair_b = together(near(mine_2, "r2_near", "dz"), near(mine_b, "cb_near", "dy"))
    t_1a = tile(pos, rows_1, cols_a, 0, jnp.bfloat16, n_out=2)
    low_1, high_1 = moved(t_1a[0], "x_1a", dx=1), moved(t_1a[1], "x_1a", dx=-1)
    own_1 = tile(pos, rows_1, cols_a, 1, jnp.float32)
    most_b = swapped(jnp.concatenate([mine_b, *pair_b]), MOST, "cb_core")
    pair_2, pair_b, _ = together(pair_2, pair_b, t_1a)
    ends_2, ends_b = together(far(pair_2, "r2_far", "dz", 2), far(pair_b, "cb_far", "dy", 1))
    rows_2 = row_places(mine_2, pair_2, ends_2)
    cols_b = most_b + swapped(jnp.concatenate(ends_b), REST, "cb_core")

    def first(ops, *waits):
        return [(after(ops[0][0], *waits), ops[0][1]), *ops[1:]]

    t_2a = tile(pos, first(rows_2, own_1), cols_a, 0, jnp.bfloat16, n_out=2)
    low_2, high_2 = moved(t_2a[0], "x_2a", dx=1), moved(t_2a[1], "x_2a", dx=-1)
    t_1b = tile(pos, first(rows_1, *t_2a), cols_b, 0, jnp.bfloat16, added=0, more=(low_1,))
    x_1b = moved(t_1b, "x_1b", dx=1)
    t_1c = tile(pos, first(rows_1, t_1b), cols_b, 1, jnp.bfloat16, added=1, more=(high_1,))
    x_1c = moved(t_1c, "x_1c", dx=-1)
    t_2b = tile(pos, first(rows_2, t_1c), cols_b, 0, jnp.bfloat16, added=0, more=(low_2,))
    x_2b = moved(t_2b, "x_2b", dx=1)
    t_2c = tile(pos, first(rows_2, t_2b), cols_b, 1, jnp.bfloat16, added=1, more=(high_2,))
    x_2c = moved(t_2c, "x_2c", dx=-1)
    own_2 = tile(pos, first(rows_2, t_2c), cols_a, 1, jnp.float32)

    gap = band_lookup(conduction_band, eps_conduction) - band_lookup(valence_band, eps_valence)
    done = finish(pos, 0, after(own_1, own_2), x_1b, x_1c, gap)
    return finish(pos, 1, own_2, x_2b, x_2c, gap, before=done)


def solution(mesh):
    placed = (
        P(None, ("wide", "narrow"), None),
        P(("wide", "narrow")),
        P(),
        P(),
        P(),
        P("narrow"),
        P("narrow"),
    )
    return jax.shard_map(
        per_device, mesh=mesh, in_specs=placed, out_specs=P(None, "narrow", "wide"), check_vma=False
    )
```

```python
import functools

import jax
import jax.numpy as jnp
from jax import lax
from jax.experimental import pallas as pl
from jax.experimental.pallas import tpu as pltpu
from jax.sharding import PartitionSpec as P

AXES = ("wide", "narrow")
SIDE = 4
BLOCK = 384
WIDTH = 2
CUTS = (0, 512, 768)
STEPS = ((2, 1, 3), (0,))


def moved(value, name, dx=0, dy=0, dz=0, core=0, per_core_z=None):
    pairs = []
    for x in range(SIDE):
        for z in range(SIDE):
            for y in range(SIDE):
                for c in range(2):
                    step = dz if per_core_z is None else per_core_z[c]
                    to = ((x + dx) % SIDE, (z + step) % SIDE, (y + dy) % SIDE, (c + core) % 2)
                    pairs.append(
                        (((x * SIDE + z) * SIDE + y) * 2 + c, ((to[0] * SIDE + to[1]) * SIDE + to[2]) * 2 + to[3])
                    )
    with jax.named_scope(name):
        return lax.ppermute(value, AXES, pairs)


def after(value, *others):
    return lax.optimization_barrier((value, *others))[0]


def prepare_kernel(pos, own, sib, weight, *outs):
    x, y, z, c = pos[0], pos[1], pos[2], pos[3]
    first = c == 0

    def piece(index):
        cut = pl.ds(pl.multiple_of(index * BLOCK, BLOCK), BLOCK)
        mine = own[:, :, cut].astype(jnp.float32)
        other = sib[:, :, cut].astype(jnp.float32)
        zero = jnp.where(first, mine, other)
        one = jnp.where(first, other, mine)
        rows = jnp.concatenate([zero[0], one[0], zero[1], one[1]], axis=0)
        scale = jnp.concatenate([weight[...]] * (BLOCK // 128), axis=1)
        return (rows * scale).astype(jnp.bfloat16)

    at = 0
    for d in range(SIDE):
        for i in range(WIDTH):
            outs[at][:, i * BLOCK : (i + 1) * BLOCK] = piece((2 * lax.rem(y + d, SIDE) + c) * WIDTH + i)
        at += 1
    for part in range(2):
        for chunk in (STEPS[0] + STEPS[1],):
            for n, delta in enumerate(chunk):
                step = 1 + 2 * c if part == 0 else 2 * c
                outs[at][n] = piece(lax.rem(x + delta, SIDE) * SIDE + lax.rem(z + step, SIDE))
            at += 1


def prepare(pos, own, sib, weight):
    rows = own.shape[1] * 4
    shapes = [jax.ShapeDtypeStruct((rows, WIDTH * BLOCK), jnp.bfloat16)] * SIDE
    shapes += [jax.ShapeDtypeStruct((SIDE, rows, BLOCK), jnp.bfloat16)] * 2
    vmem = pl.BlockSpec(memory_space=pltpu.VMEM)
    return pl.pallas_call(
        prepare_kernel,
        out_shape=shapes,
        in_specs=[pl.BlockSpec(memory_space=pltpu.SMEM), vmem, vmem, vmem],
        out_specs=[vmem] * len(shapes),
        compiler_params=pltpu.CompilerParams(vmem_limit_bytes=20 * 2**20),
        cost_estimate=pl.CostEstimate(flops=10**6, bytes_accessed=6 * 10**6, transcendentals=0),
        name="prepare",
    )(pos, own, sib, weight)


def tile_kernel(plan, pos, *refs):
    row_places, col_places, col_at, depth, n_out, added = plan
    n_row, n_col = len(row_places), len(col_places)
    row_refs, refs = refs[:n_row], refs[n_row:]
    col_refs, refs = refs[:n_col], refs[n_col:]
    if added is not None:
        more, refs = refs[0], refs[1:]
    outs, (rbuf, cbuf, acc) = refs[:n_out], refs[n_out:]
    c = pos[3]

    def take_rows(zwant):
        for ref, places in zip(row_refs, row_places):
            for index, zpos, ypos in places:
                if zpos == zwant:
                    rbuf[ypos * depth : (ypos + 1) * depth] = ref[index]

    for k in range(SIDE):
        pl.when(c == 0)(functools.partial(take_rows, k))
        pl.when(c == 1)(functools.partial(take_rows, SIDE - 1 - k))
        for ref, places in zip(col_refs, col_places):
            for index, zpos, ypos in places:
                if zpos == k:
                    value = ref[index, col_at]
                    at = slice(ypos * depth, (ypos + 1) * depth)
                    cbuf[at, :BLOCK] = value
                    value = value.astype(jnp.float32)
                    turned = jnp.concatenate([value[depth // 2 :], -value[: depth // 2]], axis=0)
                    cbuf[at, BLOCK:] = turned.astype(jnp.bfloat16)
        for m in range(0, rbuf.shape[1], 128):
            part = lax.dot_general(
                rbuf[:, m : m + 128], cbuf[...], (((0,), (0,)), ((), ())), preferred_element_type=jnp.float32
            )
            if k == 0:
                acc[m : m + 128] = part
            elif k < SIDE - 1:
                acc[m : m + 128] += part
            else:
                part = 2.0 * (acc[m : m + 128] + part)
                for p in range(2):
                    value = part[:, p * BLOCK : (p + 1) * BLOCK]
                    if added == p:
                        value = value + more[m : m + 128].astype(jnp.float32)
                    if n_out == 2:
                        outs[p][m : m + 128] = value.astype(outs[p].dtype)
                    else:
                        outs[0][p, m : m + 128] = value.astype(outs[0].dtype)


def tile(pos, row_ops, col_ops, col_at, out_dtype, n_out=1, added=None, more=()):
    depth = row_ops[0][0].shape[-2]
    rows = row_ops[0][0].shape[-1]
    plan = ([p for _, p in row_ops], [p for _, p in col_ops], col_at, depth, n_out, added)
    vmem = pl.BlockSpec(memory_space=pltpu.VMEM)
    group = SIDE * depth
    if n_out == 2:
        shapes = [jax.ShapeDtypeStruct((rows, BLOCK), out_dtype)] * 2
    else:
        shapes = jax.ShapeDtypeStruct((2, rows, BLOCK), out_dtype)
    return pl.pallas_call(
        functools.partial(tile_kernel, plan),
        out_shape=shapes,
        in_specs=[pl.BlockSpec(memory_space=pltpu.SMEM)] + [vmem] * (len(row_ops) + len(col_ops) + len(more)),
        out_specs=[vmem] * 2 if n_out == 2 else vmem,
        scratch_shapes=[
            pltpu.VMEM((group, rows), jnp.bfloat16),
            pltpu.VMEM((group, 2 * BLOCK), jnp.bfloat16),
            pltpu.VMEM((rows, 2 * BLOCK), jnp.float32),
        ],
        compiler_params=pltpu.CompilerParams(vmem_limit_bytes=16 * 2**20),
        cost_estimate=pl.CostEstimate(
            flops=40 * SIDE * group * rows * BLOCK,
            bytes_accessed=2 * SIDE * group * (rows + BLOCK),
            transcendentals=0,
        ),
        name="tile",
    )(pos, *[a for a, _ in row_ops], *[a for a, _ in col_ops], *more)


def finish_kernel(first_row, pos, own, low, high, gap, *refs):
    out = refs[-1]
    rows = own.shape[1]
    row = lax.broadcasted_iota(jnp.int32, (rows, BLOCK), 0) + (2 * pos[1] + pos[3]) * WIDTH * BLOCK + first_row
    col = lax.broadcasted_iota(jnp.int32, (rows, BLOCK), 1) + (pos[0] * SIDE + pos[2]) * BLOCK
    real = own[0] + low[0].astype(jnp.float32) + high[0].astype(jnp.float32)
    out[0] = real + jnp.where(row == col, gap[...], 0.0)
    out[1] = own[1] + low[1].astype(jnp.float32) + high[1].astype(jnp.float32)


def finish(pos, first_row, own, low, high, gap, before=None):
    rows = own.shape[1]
    at = first_row // rows
    planes = pl.BlockSpec((2, rows, BLOCK), lambda i: (0, 0, 0))
    return pl.pallas_call(
        functools.partial(finish_kernel, first_row),
        grid=(1,),
        out_shape=jax.ShapeDtypeStruct((2, WIDTH * BLOCK, BLOCK), jnp.float32),
        in_specs=[pl.BlockSpec(memory_space=pltpu.SMEM)]
        + [planes] * 3
        + [pl.BlockSpec((rows, 1), lambda i: (at, 0))]
        + ([] if before is None else [pl.BlockSpec(memory_space=pl.ANY)]),
        out_specs=pl.BlockSpec((2, rows, BLOCK), lambda i: (0, at, 0)),
        input_output_aliases={} if before is None else {5: 0},
        compiler_params=pltpu.CompilerParams(vmem_limit_bytes=16 * 2**20),
        cost_estimate=pl.CostEstimate(flops=10**6, bytes_accessed=5 * 10**6, transcendentals=0),
        name="finish",
    )(pos, own, low, high, gap[:, None], *(() if before is None else (before,)))


def band_lookup(band_ids, table):
    levels = jnp.arange(table.shape[0], dtype=jnp.int32)
    onehot_mask = band_ids[:, None] == levels[None, :]
    return jnp.sum(jnp.where(onehot_mask, table[None, :], 0.0), axis=1)


def near(mine, name, axis):
    return [moved(mine, name, **{axis: step}) for step in (1, -1)]


def far(pair, name, axis, cut):
    return [moved(pair[0][:cut], name, **{axis: 1}), moved(pair[1][cut:], name, **{axis: -1})]


def swapped(held, places, name):
    return [(held, places), (moved(held, name, core=1), [(k, SIDE - 1 - zp, yp) for k, zp, yp in places])]


def row_places(mine, pair, ends):
    return [
        (mine, [(k, 0, k) for k in range(4)]),
        (pair[0], [(k, 1, k) for k in range(4)]),
        (pair[1], [(k, 2, k) for k in range(4)]),
        (ends[0], [(k, 3, k) for k in range(2)]),
        (ends[1], [(k, 3, k + 2) for k in range(2)]),
    ]


MOST = [(2 * n + k, 1 - k, n) for n in range(3) for k in range(2)]
REST = [(0, 1, 3), (1, 0, 3)]


def together(*groups):
    flat = lax.optimization_barrier(tuple(a for group in groups for a in group))
    result, at = [], 0
    for group in groups:
        result.append(list(flat[at : at + len(group)]))
        at += len(group)
    return result


def per_device(
    pair_density, g_index, coulomb_table, eps_valence, eps_conduction, valence_band, conduction_band
):
    wide_pos, narrow_pos = lax.axis_index("wide"), lax.axis_index("narrow")
    x, z = wide_pos // SIDE, wide_pos % SIDE
    y, c = narrow_pos // 2, narrow_pos % 2
    pos = jnp.stack([x, y, z, c]).astype(jnp.int32)

    sib = moved(pair_density, "swap", core=1)
    sib_index = moved(g_index, "swap_index", core=1)
    chip_index = jnp.where(c == 0, jnp.stack([g_index, sib_index]), jnp.stack([sib_index, g_index]))
    weight = jnp.sqrt(jnp.take(coulomb_table, chip_index.reshape(-1)))
    weight = jnp.broadcast_to(jnp.concatenate([weight, weight])[:, None], (4 * g_index.shape[0], 128))
    pieces = prepare(pos, pair_density, sib, weight)
    mine_r = pieces[:SIDE]
    cols0, cols1 = pieces[SIDE:]

    f1, f3, f2 = (moved(mine_r[k], f"r_y{k}", dy=step) for k, step in ((1, 1), (3, -1), (2, 2)))
    e0 = moved(cols0, "c_z1", per_core_z=(1, -1))
    e1 = moved(cols1, "c_z2", per_core_z=(0, 2))
    (f1, f2, f3), (e0, e1) = together((f1, f2, f3), (e0, e1))
    mine_1, mine_2 = (
        jnp.stack([a[:, CUTS[i] : CUTS[i + 1]] for a in (mine_r[0], f1, f3, f2)]) for i in range(2)
    )
    mine_a, mine_b = (jnp.stack([e0[k], e1[k]]) for k in (slice(0, 3), slice(3, 4)))

    pair_1, pair_a = together(near(mine_1, "r1_near", "dz"), near(mine_a, "ca_near", "dy"))
    most_a = swapped(jnp.concatenate([mine_a, *pair_a]), MOST, "ca_core")
    ends_1, ends_a, (most_a[1],) = together(
        far(pair_1, "r1_far", "dz", 2), far(pair_a, "ca_far", "dy", 1), (most_a[1][0],)
    )
    most_a = [most_a[0], (most_a[1], [(k, SIDE - 1 - zp, yp) for k, zp, yp in MOST])]
    cols_a = most_a + swapped(jnp.concatenate(ends_a), REST, "ca_core")
    rows_1 = row_places(mine_1, pair_1, ends_1)
    mine_2, mine_b = (after(a, *ends_1, *ends_a) for a in (mine_2, mine_b))
    pair_2, pair_b = near(mine_2, "r2_near", "dz"), near(mine_b, "cb_near", "dy")

    def first(ops, *waits):
        return [(after(ops[0][0], *waits), ops[0][1]), *ops[1:]]

    def start(rows, *waits):
        t_a = tile(pos, first(rows, *waits) if waits else rows, cols_a, 0, jnp.bfloat16, n_out=2)
        return t_a, moved(t_a[0], "x_a", dx=1), moved(t_a[1], "x_a", dx=-1)

    def rest(rows, t_a, low, high):
        t_b = tile(pos, first(rows, *t_a), cols_a, 1, jnp.float32)
        t_c = tile(pos, first(rows, t_b), cols_a, 2, jnp.float32)
        t_b = jnp.stack([t_b[0] + low.astype(jnp.float32), t_b[1]]).astype(jnp.bfloat16)
        t_c = jnp.stack([t_c[0], t_c[1] + high.astype(jnp.float32)]).astype(jnp.bfloat16)
        return moved(t_b, "x_b", dx=1), moved(t_c, "x_c", dx=-1), (t_b, t_c)

    t_1a, low_1, high_1 = start(rows_1)
    pair_2, pair_b, _ = together(pair_2, pair_b, t_1a)
    ends_2 = far(pair_2, "r2_far", "dz", 2)
    rows_2 = row_places(mine_2, pair_2, ends_2)
    ends_b = far([after(a, low_1, high_1) for a in pair_b], "cb_far", "dy", 1)
    cols_b = swapped(jnp.concatenate([mine_b, *pair_b, *ends_b]), MOST + [(k + 6, zp, yp) for k, zp, yp in REST], "cb_core")
    x_1b, x_1c, t_1 = rest(rows_1, t_1a, low_1, high_1)
    t_2a, low_2, high_2 = start(rows_2, *t_1)
    x_2b, x_2c, t_2 = rest(rows_2, t_2a, low_2, high_2)
    own_1 = tile(pos, first(rows_1, *t_2), cols_b, 0, jnp.float32)
    own_2 = tile(pos, first(rows_2, own_1), cols_b, 0, jnp.float32)

    gap = band_lookup(conduction_band, eps_conduction) - band_lookup(valence_band, eps_valence)
    done = finish(pos, CUTS[0], after(own_1, own_2), x_1b, x_1c, gap)
    return finish(pos, CUTS[1], own_2, x_2b, x_2c, gap, before=done)


def solution(mesh):
    placed = (
        P(None, ("wide", "narrow"), None),
        P(("wide", "narrow")),
        P(),
        P(),
        P(),
        P("narrow"),
        P("narrow"),
    )
    return jax.shard_map(
        per_device, mesh=mesh, in_specs=placed, out_specs=P(None, "narrow", "wide"), check_vma=False
    )
```

```python
import functools

import jax
import jax.numpy as jnp
from jax import lax
from jax.experimental import pallas as pl
from jax.experimental.pallas import tpu as pltpu
from jax.sharding import PartitionSpec as P

AXES = ("wide", "narrow")
SIDE = 4
BLOCK = 384
WIDTH = 2
CUTS = (0, 512, 768)
STEPS = ((2, 1, 3), (0,))


def moved(value, name, dx=0, dy=0, dz=0, core=0, per_core_z=None, flip_y=0):
    pairs = []
    for x in range(SIDE):
        for z in range(SIDE):
            for y in range(SIDE):
                for c in range(2):
                    step = dz if per_core_z is None else per_core_z[c]
                    to = ((x + dx) % SIDE, (z + step) % SIDE, ((y ^ flip_y) + dy) % SIDE, (c + core) % 2)
                    pairs.append(
                        (((x * SIDE + z) * SIDE + y) * 2 + c, ((to[0] * SIDE + to[1]) * SIDE + to[2]) * 2 + to[3])
                    )
    with jax.named_scope(name):
        return lax.ppermute(value, AXES, pairs)


def after(value, *others):
    return lax.optimization_barrier((value, *others))[0]


def prepare_kernel(pos, own, sib, weight, *outs):
    x, y, z, c = pos[0], pos[1], pos[2], pos[3]
    first = c == 0

    def piece(index):
        cut = pl.ds(pl.multiple_of(index * BLOCK, BLOCK), BLOCK)
        mine = own[:, :, cut].astype(jnp.float32)
        other = sib[:, :, cut].astype(jnp.float32)
        zero = jnp.where(first, mine, other)
        one = jnp.where(first, other, mine)
        rows = jnp.concatenate([zero[0], one[0], zero[1], one[1]], axis=0)
        scale = jnp.concatenate([weight[...]] * (BLOCK // 128), axis=1)
        return (rows * scale).astype(jnp.bfloat16)

    at = 0
    for d in range(SIDE):
        for i in range(WIDTH):
            outs[at][:, i * BLOCK : (i + 1) * BLOCK] = piece((2 * lax.rem(y + d, SIDE) + c) * WIDTH + i)
        at += 1
    for part in range(2):
        for chunk in (STEPS[0] + STEPS[1],):
            for n, delta in enumerate(chunk):
                step = 1 + 2 * c if part == 0 else 2 * c
                outs[at][n] = piece(lax.rem(x + delta, SIDE) * SIDE + lax.rem(z + step, SIDE))
            at += 1


def prepare(pos, own, sib, weight):
    rows = own.shape[1] * 4
    shapes = [jax.ShapeDtypeStruct((rows, WIDTH * BLOCK), jnp.bfloat16)] * SIDE
    shapes += [jax.ShapeDtypeStruct((SIDE, rows, BLOCK), jnp.bfloat16)] * 2
    vmem = pl.BlockSpec(memory_space=pltpu.VMEM)
    return pl.pallas_call(
        prepare_kernel,
        out_shape=shapes,
        in_specs=[pl.BlockSpec(memory_space=pltpu.SMEM), vmem, vmem, vmem],
        out_specs=[vmem] * len(shapes),
        compiler_params=pltpu.CompilerParams(vmem_limit_bytes=20 * 2**20),
        cost_estimate=pl.CostEstimate(flops=10**6, bytes_accessed=6 * 10**6, transcendentals=0),
        name="prepare",
    )(pos, own, sib, weight)


def tile_kernel(plan, pos, *refs):
    row_places, col_places, col_at, depth, n_out, added = plan
    n_row, n_col = len(row_places), len(col_places)
    row_refs, refs = refs[:n_row], refs[n_row:]
    col_refs, refs = refs[:n_col], refs[n_col:]
    if added is not None:
        more, refs = refs[0], refs[1:]
    outs, (rbuf, cbuf, acc) = refs[:n_out], refs[n_out:]
    c = pos[3]

    def take_rows(zwant):
        for ref, places in zip(row_refs, row_places):
            for index, zpos, ypos in places:
                if zpos == zwant:
                    rbuf[ypos * depth : (ypos + 1) * depth] = ref[index]

    for k in range(SIDE):
        pl.when(c == 0)(functools.partial(take_rows, k))
        pl.when(c == 1)(functools.partial(take_rows, SIDE - 1 - k))
        for ref, places in zip(col_refs, col_places):
            for index, zpos, ypos in places:
                if zpos == k:
                    value = ref[index, col_at]
                    if callable(ypos):
                        at = pl.ds(pl.multiple_of(ypos(pos[1]) * depth, depth), depth)
                    else:
                        at = slice(ypos * depth, (ypos + 1) * depth)
                    cbuf[at, :BLOCK] = value
                    value = value.astype(jnp.float32)
                    turned = jnp.concatenate([value[depth // 2 :], -value[: depth // 2]], axis=0)
                    cbuf[at, BLOCK:] = turned.astype(jnp.bfloat16)
        for m in range(0, rbuf.shape[1], 128):
            part = lax.dot_general(
                rbuf[:, m : m + 128], cbuf[...], (((0,), (0,)), ((), ())), preferred_element_type=jnp.float32
            )
            if k == 0:
                acc[m : m + 128] = part
            elif k < SIDE - 1:
                acc[m : m + 128] += part
            else:
                part = 2.0 * (acc[m : m + 128] + part)
                for p in range(2):
                    value = part[:, p * BLOCK : (p + 1) * BLOCK]
                    if added == p:
                        value = value + more[m : m + 128].astype(jnp.float32)
                    if n_out == 2:
                        outs[p][m : m + 128] = value.astype(outs[p].dtype)
                    else:
                        outs[0][p, m : m + 128] = value.astype(outs[0].dtype)


def tile(pos, row_ops, col_ops, col_at, out_dtype, n_out=1, added=None, more=()):
    depth = row_ops[0][0].shape[-2]
    rows = row_ops[0][0].shape[-1]
    plan = ([p for _, p in row_ops], [p for _, p in col_ops], col_at, depth, n_out, added)
    vmem = pl.BlockSpec(memory_space=pltpu.VMEM)
    group = SIDE * depth
    if n_out == 2:
        shapes = [jax.ShapeDtypeStruct((rows, BLOCK), out_dtype)] * 2
    else:
        shapes = jax.ShapeDtypeStruct((2, rows, BLOCK), out_dtype)
    return pl.pallas_call(
        functools.partial(tile_kernel, plan),
        out_shape=shapes,
        in_specs=[pl.BlockSpec(memory_space=pltpu.SMEM)] + [vmem] * (len(row_ops) + len(col_ops) + len(more)),
        out_specs=[vmem] * 2 if n_out == 2 else vmem,
        scratch_shapes=[
            pltpu.VMEM((group, rows), jnp.bfloat16),
            pltpu.VMEM((group, 2 * BLOCK), jnp.bfloat16),
            pltpu.VMEM((rows, 2 * BLOCK), jnp.float32),
        ],
        compiler_params=pltpu.CompilerParams(vmem_limit_bytes=16 * 2**20),
        cost_estimate=pl.CostEstimate(
            flops=1000,
            bytes_accessed=1000,
            transcendentals=0,
        ),
        name="tile",
    )(pos, *[a for a, _ in row_ops], *[a for a, _ in col_ops], *more)


def finish_kernel(first_row, pos, own, low, high, gap, *refs):
    out = refs[-1]
    rows = own.shape[1]
    row = lax.broadcasted_iota(jnp.int32, (rows, BLOCK), 0) + (2 * pos[1] + pos[3]) * WIDTH * BLOCK + first_row
    col = lax.broadcasted_iota(jnp.int32, (rows, BLOCK), 1) + (pos[0] * SIDE + pos[2]) * BLOCK
    real = own[0] + low[0].astype(jnp.float32) + high[0].astype(jnp.float32)
    out[0] = real + jnp.where(row == col, gap[...], 0.0)
    out[1] = own[1] + low[1].astype(jnp.float32) + high[1].astype(jnp.float32)


def finish(pos, first_row, own, low, high, gap, before=None):
    rows = own.shape[1]
    at = first_row // rows
    planes = pl.BlockSpec((2, rows, BLOCK), lambda i: (0, 0, 0))
    return pl.pallas_call(
        functools.partial(finish_kernel, first_row),
        grid=(1,),
        out_shape=jax.ShapeDtypeStruct((2, WIDTH * BLOCK, BLOCK), jnp.float32),
        in_specs=[pl.BlockSpec(memory_space=pltpu.SMEM)]
        + [planes] * 3
        + [pl.BlockSpec((rows, 1), lambda i: (at, 0))]
        + ([] if before is None else [pl.BlockSpec(memory_space=pl.ANY)]),
        out_specs=pl.BlockSpec((2, rows, BLOCK), lambda i: (0, at, 0)),
        input_output_aliases={} if before is None else {5: 0},
        compiler_params=pltpu.CompilerParams(vmem_limit_bytes=16 * 2**20),
        cost_estimate=pl.CostEstimate(flops=10**6, bytes_accessed=5 * 10**6, transcendentals=0),
        name="finish",
    )(pos, own, low, high, gap[:, None], *(() if before is None else (before,)))


def band_lookup(band_ids, table):
    levels = jnp.arange(table.shape[0], dtype=jnp.int32)
    onehot_mask = band_ids[:, None] == levels[None, :]
    return jnp.sum(jnp.where(onehot_mask, table[None, :], 0.0), axis=1)


def near(mine, name, axis):
    return [moved(mine, name, **{axis: step}) for step in (1, -1)]


def far(pair, name, axis, cut):
    return [moved(pair[0][:cut], name, **{axis: 1}), moved(pair[1][cut:], name, **{axis: -1})]


def swapped(held, places, name):
    return [(held, places), (moved(held, name, core=1), [(k, SIDE - 1 - zp, yp) for k, zp, yp in places])]


def row_places(mine, pair, ends):
    return [
        (mine, [(k, 0, k) for k in range(4)]),
        (pair[0], [(k, 1, k) for k in range(4)]),
        (pair[1], [(k, 2, k) for k in range(4)]),
        (ends[0], [(k, 3, k) for k in range(2)]),
        (ends[1], [(k, 3, k + 2) for k in range(2)]),
    ]


MOST = [(2 * n + k, 1 - k, n) for n in range(3) for k in range(2)]
REST = [(0, 1, 3), (1, 0, 3)]
FLIPS = (0, lambda y: 2 - lax.rem(y, 2), 3, lambda y: 1 + lax.rem(y, 2))
FLIPPED = [(2 * n + k, 1 - k, at) for n, at in enumerate(FLIPS) for k in range(2)]


def together(*groups):
    flat = lax.optimization_barrier(tuple(a for group in groups for a in group))
    result, at = [], 0
    for group in groups:
        result.append(list(flat[at : at + len(group)]))
        at += len(group)
    return result


def per_device(
    pair_density, g_index, coulomb_table, eps_valence, eps_conduction, valence_band, conduction_band
):
    wide_pos, narrow_pos = lax.axis_index("wide"), lax.axis_index("narrow")
    x, z = wide_pos // SIDE, wide_pos % SIDE
    y, c = narrow_pos // 2, narrow_pos % 2
    pos = jnp.stack([x, y, z, c]).astype(jnp.int32)

    sib = moved(pair_density, "swap", core=1)
    sib_index = moved(g_index, "swap_index", core=1)
    chip_index = jnp.where(c == 0, jnp.stack([g_index, sib_index]), jnp.stack([sib_index, g_index]))
    weight = jnp.sqrt(jnp.take(coulomb_table, chip_index.reshape(-1)))
    weight = jnp.broadcast_to(jnp.concatenate([weight, weight])[:, None], (4 * g_index.shape[0], 128))
    pieces = prepare(pos, pair_density, sib, weight)
    mine_r = pieces[:SIDE]
    cols0, cols1 = pieces[SIDE:]

    f1, f3, f2 = (moved(mine_r[k], f"r_y{k}", dy=step) for k, step in ((1, 1), (3, -1), (2, 2)))
    e0 = moved(cols0, "c_z1", per_core_z=(1, -1))
    e1 = moved(cols1, "c_z2", per_core_z=(0, 2))
    (f1, f2, f3), (e0, e1) = together((f1, f2, f3), (e0, e1))
    mine_1, mine_2 = (
        jnp.stack([a[:, CUTS[i] : CUTS[i + 1]] for a in (mine_r[0], f1, f3, f2)]) for i in range(2)
    )
    mine_a, mine_b = (jnp.stack([e0[k], e1[k]]) for k in (slice(0, 3), slice(3, 4)))

    pair_1, pair_a = together(near(mine_1, "r1_near", "dz"), near(mine_a, "ca_near", "dy"))
    most_a = swapped(jnp.concatenate([mine_a, *pair_a]), MOST, "ca_core")
    ends_1, ends_a, (most_a[1],) = together(
        far(pair_1, "r1_far", "dz", 2), far(pair_a, "ca_far", "dy", 1), (most_a[1][0],)
    )
    most_a = [most_a[0], (most_a[1], [(k, SIDE - 1 - zp, yp) for k, zp, yp in MOST])]
    cols_a = most_a + swapped(jnp.concatenate(ends_a), REST, "ca_core")
    rows_1 = row_places(mine_1, pair_1, ends_1)
    mine_2, mine_b = (after(a, *ends_1, *ends_a) for a in (mine_2, mine_b))
    pair_2 = near(mine_2, "r2_near", "dz")
    two_b = jnp.concatenate([mine_b, moved(mine_b, "cb_one", flip_y=1)])

    def first(ops, *waits):
        return [(after(ops[0][0], *waits), ops[0][1]), *ops[1:]]

    def start(rows, *waits):
        t_a = tile(pos, first(rows, *waits) if waits else rows, cols_a, 0, jnp.bfloat16, n_out=2)
        return t_a, moved(t_a[0], "x_a", dx=1), moved(t_a[1], "x_a", dx=-1)

    def send(t_b, t_c, low, high):
        t_b = jnp.stack([t_b[0] + low.astype(jnp.float32), t_b[1]]).astype(jnp.bfloat16)
        t_c = jnp.stack([t_c[0], t_c[1] + high.astype(jnp.float32)]).astype(jnp.bfloat16)
        return moved(t_b, "x_b", dx=1), moved(t_c, "x_c", dx=-1), (t_b, t_c)

    t_1a, low_1, high_1 = start(rows_1)
    pair_2, (two_b,), t_1a = together(pair_2, (two_b,), t_1a)
    more_b = moved(two_b, "cb_two", flip_y=2)
    ends_2 = far(pair_2, "r2_far", "dz", 2)
    rows_2 = row_places(mine_2, pair_2, ends_2)
    t_1b = tile(pos, first(rows_1, *t_1a, *pair_2, two_b), cols_a, 1, jnp.float32)
    t_1c = tile(pos, first(rows_1, t_1b), cols_a, 2, jnp.float32)
    x_1b, x_1c, t_1 = send(t_1b, t_1c, low_1, high_1)
    t_2a, low_2, high_2 = start(rows_2, *t_1)
    cols_b = swapped(jnp.concatenate([two_b, more_b]), FLIPPED, "cb_core")
    t_2b = tile(pos, first(rows_2, *t_2a), cols_a, 1, jnp.float32)
    t_2c = tile(pos, first(rows_2, t_2b), cols_a, 2, jnp.float32)
    t_2c_raw = t_2c
    t_2b, t_2c = (after(t, x_1b, x_1c) for t in (t_2b, t_2c))
    x_2b, x_2c, t_2 = send(t_2b, t_2c, low_2, high_2)
    own_1 = tile(pos, first(rows_1, t_2c_raw), cols_b, 0, jnp.float32)
    own_2 = tile(pos, first(rows_2, own_1), cols_b, 0, jnp.float32)

    gap = band_lookup(conduction_band, eps_conduction) - band_lookup(valence_band, eps_valence)
    done = finish(pos, CUTS[0], after(own_1, own_2), x_1b, x_1c, gap)
    return finish(pos, CUTS[1], own_2, x_2b, x_2c, gap, before=done)


def solution(mesh):
    placed = (
        P(None, ("wide", "narrow"), None),
        P(("wide", "narrow")),
        P(),
        P(),
        P(),
        P("narrow"),
        P("narrow"),
    )
    return jax.shard_map(
        per_device, mesh=mesh, in_specs=placed, out_specs=P(None, "narrow", "wide"), check_vma=False
    )
```

```python
import functools

import jax
import jax.numpy as jnp
from jax import lax
from jax.experimental import pallas as pl
from jax.experimental.pallas import tpu as pltpu
from jax.sharding import PartitionSpec as P

AXES = ("wide", "narrow")
SIDE = 4
BLOCK = 384
WIDTH = 2
CUTS = (0, 512, 768)
STEPS = ((2, 1, 3), (0,))


def moved(value, name, dx=0, dy=0, dz=0, core=0, per_core_z=None, flip_y=0):
    pairs = []
    for x in range(SIDE):
        for z in range(SIDE):
            for y in range(SIDE):
                for c in range(2):
                    step = dz if per_core_z is None else per_core_z[c]
                    to = ((x + dx) % SIDE, (z + step) % SIDE, ((y ^ flip_y) + dy) % SIDE, (c + core) % 2)
                    pairs.append(
                        (((x * SIDE + z) * SIDE + y) * 2 + c, ((to[0] * SIDE + to[1]) * SIDE + to[2]) * 2 + to[3])
                    )
    with jax.named_scope(name):
        return lax.ppermute(value, AXES, pairs)


def after(value, *others):
    return lax.optimization_barrier((value, *others))[0]


def prepare_kernel(pos, own, sib, weight, *outs):
    x, y, z, c = pos[0], pos[1], pos[2], pos[3]
    first = c == 0

    def piece(index):
        cut = pl.ds(pl.multiple_of(index * BLOCK, BLOCK), BLOCK)
        mine = own[:, :, cut].astype(jnp.float32)
        other = sib[:, :, cut].astype(jnp.float32)
        zero = jnp.where(first, mine, other)
        one = jnp.where(first, other, mine)
        rows = jnp.concatenate([zero[0], one[0], zero[1], one[1]], axis=0)
        scale = jnp.concatenate([weight[...]] * (BLOCK // 128), axis=1)
        return (rows * scale).astype(jnp.bfloat16)

    at = 0
    for d in range(SIDE):
        for i in range(WIDTH):
            outs[at][:, i * BLOCK : (i + 1) * BLOCK] = piece((2 * lax.rem(y + d, SIDE) + c) * WIDTH + i)
        at += 1
    for part in range(2):
        for chunk in (STEPS[0] + STEPS[1],):
            for n, delta in enumerate(chunk):
                step = 1 + 2 * c if part == 0 else 2 * c
                outs[at][n] = piece(lax.rem(x + delta, SIDE) * SIDE + lax.rem(z + step, SIDE))
            at += 1


def prepare(pos, own, sib, weight):
    rows = own.shape[1] * 4
    shapes = [jax.ShapeDtypeStruct((rows, WIDTH * BLOCK), jnp.bfloat16)] * SIDE
    shapes += [jax.ShapeDtypeStruct((SIDE, rows, BLOCK), jnp.bfloat16)] * 2
    vmem = pl.BlockSpec(memory_space=pltpu.VMEM)
    return pl.pallas_call(
        prepare_kernel,
        out_shape=shapes,
        in_specs=[pl.BlockSpec(memory_space=pltpu.SMEM), vmem, vmem, vmem],
        out_specs=[vmem] * len(shapes),
        compiler_params=pltpu.CompilerParams(vmem_limit_bytes=20 * 2**20),
        cost_estimate=pl.CostEstimate(flops=10**6, bytes_accessed=6 * 10**6, transcendentals=0),
        name="prepare",
    )(pos, own, sib, weight)


def tile_kernel(plan, pos, *refs):
    row_places, col_places, col_at, depth, n_out, added = plan
    n_row, n_col = len(row_places), len(col_places)
    row_refs, refs = refs[:n_row], refs[n_row:]
    col_refs, refs = refs[:n_col], refs[n_col:]
    if added is not None:
        more, refs = refs[0], refs[1:]
    outs, (rbuf, cbuf, acc) = refs[:n_out], refs[n_out:]
    c = pos[3]

    def take_rows(zwant):
        for ref, places in zip(row_refs, row_places):
            for index, zpos, ypos in places:
                if zpos == zwant:
                    rbuf[ypos * depth : (ypos + 1) * depth] = ref[index]

    for k in range(SIDE):
        pl.when(c == 0)(functools.partial(take_rows, k))
        pl.when(c == 1)(functools.partial(take_rows, SIDE - 1 - k))
        for ref, places in zip(col_refs, col_places):
            for index, zpos, ypos in places:
                if zpos == k:
                    value = ref[index, col_at]
                    if callable(ypos):
                        at = pl.ds(pl.multiple_of(ypos(pos[1]) * depth, depth), depth)
                    else:
                        at = slice(ypos * depth, (ypos + 1) * depth)
                    cbuf[at, :BLOCK] = value
                    value = value.astype(jnp.float32)
                    turned = jnp.concatenate([value[depth // 2 :], -value[: depth // 2]], axis=0)
                    cbuf[at, BLOCK:] = turned.astype(jnp.bfloat16)
        for m in range(0, rbuf.shape[1], 128):
            part = lax.dot_general(
                rbuf[:, m : m + 128], cbuf[...], (((0,), (0,)), ((), ())), preferred_element_type=jnp.float32
            )
            if k == 0:
                acc[m : m + 128] = part
            elif k < SIDE - 1:
                acc[m : m + 128] += part
            else:
                part = 2.0 * (acc[m : m + 128] + part)
                for p in range(2):
                    value = part[:, p * BLOCK : (p + 1) * BLOCK]
                    if added == p:
                        value = value + more[m : m + 128].astype(jnp.float32)
                    if n_out == 2:
                        outs[p][m : m + 128] = value.astype(outs[p].dtype)
                    else:
                        outs[0][p, m : m + 128] = value.astype(outs[0].dtype)


def tile(pos, row_ops, col_ops, col_at, out_dtype, n_out=1, added=None, more=()):
    depth = row_ops[0][0].shape[-2]
    rows = row_ops[0][0].shape[-1]
    plan = ([p for _, p in row_ops], [p for _, p in col_ops], col_at, depth, n_out, added)
    vmem = pl.BlockSpec(memory_space=pltpu.VMEM)
    group = SIDE * depth
    if n_out == 2:
        shapes = [jax.ShapeDtypeStruct((rows, BLOCK), out_dtype)] * 2
    else:
        shapes = jax.ShapeDtypeStruct((2, rows, BLOCK), out_dtype)
    return pl.pallas_call(
        functools.partial(tile_kernel, plan),
        out_shape=shapes,
        in_specs=[pl.BlockSpec(memory_space=pltpu.SMEM)] + [vmem] * (len(row_ops) + len(col_ops) + len(more)),
        out_specs=[vmem] * 2 if n_out == 2 else vmem,
        scratch_shapes=[
            pltpu.VMEM((group, rows), jnp.bfloat16),
            pltpu.VMEM((group, 2 * BLOCK), jnp.bfloat16),
            pltpu.VMEM((rows, 2 * BLOCK), jnp.float32),
        ],
        compiler_params=pltpu.CompilerParams(vmem_limit_bytes=16 * 2**20),
        cost_estimate=pl.CostEstimate(
            flops=1000,
            bytes_accessed=1000,
            transcendentals=0,
        ),
        name="tile",
    )(pos, *[a for a, _ in row_ops], *[a for a, _ in col_ops], *more)


def finish_kernel(first_row, pos, own, low, high, gap, *refs):
    out = refs[-1]
    rows = own.shape[1]
    row = lax.broadcasted_iota(jnp.int32, (rows, BLOCK), 0) + (2 * pos[1] + pos[3]) * WIDTH * BLOCK + first_row
    col = lax.broadcasted_iota(jnp.int32, (rows, BLOCK), 1) + (pos[0] * SIDE + pos[2]) * BLOCK
    real = own[0] + low[0].astype(jnp.float32) + high[0].astype(jnp.float32)
    out[0] = real + jnp.where(row == col, gap[...], 0.0)
    out[1] = own[1] + low[1].astype(jnp.float32) + high[1].astype(jnp.float32)


def finish(pos, first_row, own, low, high, gap, before=None):
    rows = own.shape[1]
    at = first_row // rows
    planes = pl.BlockSpec((2, rows, BLOCK), lambda i: (0, 0, 0))
    return pl.pallas_call(
        functools.partial(finish_kernel, first_row),
        grid=(1,),
        out_shape=jax.ShapeDtypeStruct((2, WIDTH * BLOCK, BLOCK), jnp.float32),
        in_specs=[pl.BlockSpec(memory_space=pltpu.SMEM)]
        + [planes] * 3
        + [pl.BlockSpec((rows, 1), lambda i: (at, 0))]
        + ([] if before is None else [pl.BlockSpec(memory_space=pl.ANY)]),
        out_specs=pl.BlockSpec((2, rows, BLOCK), lambda i: (0, at, 0)),
        input_output_aliases={} if before is None else {5: 0},
        compiler_params=pltpu.CompilerParams(vmem_limit_bytes=16 * 2**20),
        cost_estimate=pl.CostEstimate(flops=10**6, bytes_accessed=5 * 10**6, transcendentals=0),
        name="finish",
    )(pos, own, low, high, gap[:, None], *(() if before is None else (before,)))


def band_lookup(band_ids, table):
    levels = jnp.arange(table.shape[0], dtype=jnp.int32)
    onehot_mask = band_ids[:, None] == levels[None, :]
    return jnp.sum(jnp.where(onehot_mask, table[None, :], 0.0), axis=1)


def near(mine, name, axis):
    return [moved(mine, name, **{axis: step}) for step in (1, -1)]


def far(pair, name, axis, cut):
    return [moved(pair[0][:cut], name, **{axis: 1}), moved(pair[1][cut:], name, **{axis: -1})]


def swapped(held, places, name):
    return [(held, places), (moved(held, name, core=1), [(k, SIDE - 1 - zp, yp) for k, zp, yp in places])]


def row_places(mine, pair, ends):
    return [
        (mine, [(k, 0, k) for k in range(4)]),
        (pair[0], [(k, 1, k) for k in range(4)]),
        (pair[1], [(k, 2, k) for k in range(4)]),
        (ends[0], [(k, 3, k) for k in range(2)]),
        (ends[1], [(k, 3, k + 2) for k in range(2)]),
    ]


MOST = [(2 * n + k, 1 - k, n) for n in range(3) for k in range(2)]
REST = [(0, 1, 3), (1, 0, 3)]
FLIPS = (0, lambda y: 2 - lax.rem(y, 2), 3, lambda y: 1 + lax.rem(y, 2))
FLIPPED = [(2 * n + k, 1 - k, at) for n, at in enumerate(FLIPS) for k in range(2)]


def together(*groups):
    flat = lax.optimization_barrier(tuple(a for group in groups for a in group))
    result, at = [], 0
    for group in groups:
        result.append(list(flat[at : at + len(group)]))
        at += len(group)
    return result


def per_device(
    pair_density, g_index, coulomb_table, eps_valence, eps_conduction, valence_band, conduction_band
):
    wide_pos, narrow_pos = lax.axis_index("wide"), lax.axis_index("narrow")
    x, z = wide_pos // SIDE, wide_pos % SIDE
    y, c = narrow_pos // 2, narrow_pos % 2
    pos = jnp.stack([x, y, z, c]).astype(jnp.int32)

    sib = moved(pair_density, "swap", core=1)
    sib_index = moved(g_index, "swap_index", core=1)
    chip_index = jnp.where(c == 0, jnp.stack([g_index, sib_index]), jnp.stack([sib_index, g_index]))
    weight = jnp.sqrt(jnp.take(coulomb_table, chip_index.reshape(-1)))
    weight = jnp.broadcast_to(jnp.concatenate([weight, weight])[:, None], (4 * g_index.shape[0], 128))
    pieces = prepare(pos, pair_density, sib, weight)
    mine_r = pieces[:SIDE]
    cols0, cols1 = pieces[SIDE:]

    f1, f3, f2 = (moved(mine_r[k], f"r_y{k}", dy=step) for k, step in ((1, 1), (3, -1), (2, 2)))
    e0 = moved(cols0, "c_z1", per_core_z=(1, -1))
    e1 = moved(cols1, "c_z2", per_core_z=(0, 2))
    (f1, f2, f3), (e0, e1) = together((f1, f2, f3), (e0, e1))
    mine_1, mine_2 = (
        jnp.stack([a[:, CUTS[i] : CUTS[i + 1]] for a in (mine_r[0], f1, f3, f2)]) for i in range(2)
    )
    mine_a, mine_b = (jnp.stack([e0[k], e1[k]]) for k in (slice(0, 3), slice(3, 4)))

    pair_1, pair_a = together(near(mine_1, "r1_near", "dz"), near(mine_a, "ca_near", "dy"))
    most_a = swapped(jnp.concatenate([mine_a, *pair_a]), MOST, "ca_core")
    ends_1, ends_a, (most_a[1],) = together(
        far(pair_1, "r1_far", "dz", 2), far(pair_a, "ca_far", "dy", 1), (most_a[1][0],)
    )
    most_a = [most_a[0], (most_a[1], [(k, SIDE - 1 - zp, yp) for k, zp, yp in MOST])]
    cols_a = most_a + swapped(jnp.concatenate(ends_a), REST, "ca_core")
    rows_1 = row_places(mine_1, pair_1, ends_1)
    mine_2, mine_b = (after(a, *ends_1, *ends_a) for a in (mine_2, mine_b))
    pair_2 = near(mine_2, "r2_near", "dz")
    two_b = jnp.concatenate([mine_b, moved(mine_b, "cb_one", flip_y=1)])

    def first(ops, *waits):
        return [(after(ops[0][0], *waits), ops[0][1]), *ops[1:]]

    def start(rows, *waits):
        t_a = tile(pos, first(rows, *waits) if waits else rows, cols_a, 0, jnp.bfloat16, n_out=2)
        return t_a, moved(t_a[0], "x_a", dx=1), moved(t_a[1], "x_a", dx=-1)

    def send(t_b, t_c, low, high):
        t_b = jnp.stack([t_b[0] + low.astype(jnp.float32), t_b[1]]).astype(jnp.bfloat16)
        t_c = jnp.stack([t_c[0], t_c[1] + high.astype(jnp.float32)]).astype(jnp.bfloat16)
        return moved(t_b, "x_b", dx=1), moved(t_c, "x_c", dx=-1), (t_b, t_c)

    t_1a, low_1, high_1 = start(rows_1)
    pair_2, (two_b,), t_1a = together(pair_2, (two_b,), t_1a)
    more_b = moved(two_b, "cb_two", flip_y=2)
    ends_2 = far(pair_2, "r2_far", "dz", 2)
    rows_2 = row_places(mine_2, pair_2, ends_2)
    t_1b = tile(pos, first(rows_1, *t_1a, *pair_2, two_b), cols_a, 1, jnp.float32)
    t_1c = tile(pos, first(rows_1, t_1b), cols_a, 2, jnp.float32)
    x_1b, x_1c, t_1 = send(t_1b, t_1c, low_1, high_1)
    t_2a, low_2, high_2 = start(rows_2, *t_1)
    cols_b = swapped(jnp.concatenate([two_b, after(more_b, t_2a[0])]), FLIPPED, "cb_core")
    t_2b = tile(pos, first(rows_2, *t_2a), cols_a, 1, jnp.float32)
    t_2c = tile(pos, first(rows_2, t_2b), cols_a, 2, jnp.float32)
    t_2c_raw = t_2c
    t_2b, t_2c = (after(t, x_1b, x_1c) for t in (t_2b, t_2c))
    x_2b, x_2c, t_2 = send(t_2b, t_2c, low_2, high_2)
    own_1 = tile(pos, first(rows_1, t_2c_raw), cols_b, 0, jnp.float32)
    own_2 = tile(pos, first(rows_2, own_1), cols_b, 0, jnp.float32)

    gap = band_lookup(conduction_band, eps_conduction) - band_lookup(valence_band, eps_valence)
    done = finish(pos, CUTS[0], after(own_1, own_2), x_1b, x_1c, gap)
    return finish(pos, CUTS[1], own_2, x_2b, x_2c, gap, before=done)


def solution(mesh):
    placed = (
        P(None, ("wide", "narrow"), None),
        P(("wide", "narrow")),
        P(),
        P(),
        P(),
        P("narrow"),
        P("narrow"),
    )
    return jax.shard_map(
        per_device, mesh=mesh, in_specs=placed, out_specs=P(None, "narrow", "wide"), check_vma=False
    )
```

```python
import functools

import jax
import jax.numpy as jnp
from jax import lax
from jax.experimental import pallas as pl
from jax.experimental.pallas import tpu as pltpu
from jax.sharding import PartitionSpec as P

AXES = ("wide", "narrow")
SIDE = 4
BLOCK = 384
WIDTH = 2
CUTS = (0, 512, 768)
STEPS = ((2, 1, 3), (0,))


def moved(value, name, dx=0, dy=0, dz=0, core=0, per_core_z=None, flip_y=0):
    pairs = []
    for x in range(SIDE):
        for z in range(SIDE):
            for y in range(SIDE):
                for c in range(2):
                    step = dz if per_core_z is None else per_core_z[c]
                    to = ((x + dx) % SIDE, (z + step) % SIDE, ((y ^ flip_y) + dy) % SIDE, (c + core) % 2)
                    pairs.append(
                        (((x * SIDE + z) * SIDE + y) * 2 + c, ((to[0] * SIDE + to[1]) * SIDE + to[2]) * 2 + to[3])
                    )
    with jax.named_scope(name):
        return lax.ppermute(value, AXES, pairs)


def after(value, *others):
    return lax.optimization_barrier((value, *others))[0]


def prepare_kernel(pos, own, sib, weight, *outs):
    x, y, z, c = pos[0], pos[1], pos[2], pos[3]
    first = c == 0

    def piece(index):
        cut = pl.ds(pl.multiple_of(index * BLOCK, BLOCK), BLOCK)
        mine = own[:, :, cut].astype(jnp.float32)
        other = sib[:, :, cut].astype(jnp.float32)
        zero = jnp.where(first, mine, other)
        one = jnp.where(first, other, mine)
        rows = jnp.concatenate([zero[0], one[0], zero[1], one[1]], axis=0)
        scale = jnp.concatenate([weight[...]] * (BLOCK // 128), axis=1)
        return (rows * scale).astype(jnp.bfloat16)

    at = 0
    for d in range(SIDE):
        for i in range(WIDTH):
            outs[at][:, i * BLOCK : (i + 1) * BLOCK] = piece((2 * lax.rem(y + d, SIDE) + c) * WIDTH + i)
        at += 1
    for part in range(2):
        for chunk in (STEPS[0] + STEPS[1],):
            for n, delta in enumerate(chunk):
                step = 1 + 2 * c if part == 0 else 2 * c
                outs[at][n] = piece(lax.rem(x + delta, SIDE) * SIDE + lax.rem(z + step, SIDE))
            at += 1


def prepare(pos, own, sib, weight):
    rows = own.shape[1] * 4
    shapes = [jax.ShapeDtypeStruct((rows, WIDTH * BLOCK), jnp.bfloat16)] * SIDE
    shapes += [jax.ShapeDtypeStruct((SIDE, rows, BLOCK), jnp.bfloat16)] * 2
    vmem = pl.BlockSpec(memory_space=pltpu.VMEM)
    return pl.pallas_call(
        prepare_kernel,
        out_shape=shapes,
        in_specs=[pl.BlockSpec(memory_space=pltpu.SMEM), vmem, vmem, vmem],
        out_specs=[vmem] * len(shapes),
        compiler_params=pltpu.CompilerParams(vmem_limit_bytes=20 * 2**20),
        cost_estimate=pl.CostEstimate(flops=10**6, bytes_accessed=6 * 10**6, transcendentals=0),
        name="prepare",
    )(pos, own, sib, weight)


def tile_kernel(plan, pos, *refs):
    row_places, col_places, col_at, depth, n_out, added = plan
    n_row, n_col = len(row_places), len(col_places)
    row_refs, refs = refs[:n_row], refs[n_row:]
    col_refs, refs = refs[:n_col], refs[n_col:]
    if added is not None:
        more, refs = refs[0], refs[1:]
    outs, (rbuf, cbuf, acc) = refs[:n_out], refs[n_out:]
    c = pos[3]

    def take_rows(zwant):
        for ref, places in zip(row_refs, row_places):
            for index, zpos, ypos in places:
                if zpos == zwant:
                    rbuf[ypos * depth : (ypos + 1) * depth] = ref[index]

    for k in range(SIDE):
        pl.when(c == 0)(functools.partial(take_rows, k))
        pl.when(c == 1)(functools.partial(take_rows, SIDE - 1 - k))
        for ref, places in zip(col_refs, col_places):
            for index, zpos, ypos in places:
                if zpos == k:
                    value = ref[index, col_at]
                    if callable(ypos):
                        at = pl.ds(pl.multiple_of(ypos(pos[1]) * depth, depth), depth)
                    else:
                        at = slice(ypos * depth, (ypos + 1) * depth)
                    cbuf[at, :BLOCK] = value
                    value = value.astype(jnp.float32)
                    turned = jnp.concatenate([value[depth // 2 :], -value[: depth // 2]], axis=0)
                    cbuf[at, BLOCK:] = turned.astype(jnp.bfloat16)
        for m in range(0, rbuf.shape[1], 128):
            part = lax.dot_general(
                rbuf[:, m : m + 128], cbuf[...], (((0,), (0,)), ((), ())), preferred_element_type=jnp.float32
            )
            if k == 0:
                acc[m : m + 128] = part
            elif k < SIDE - 1:
                acc[m : m + 128] += part
            else:
                part = 2.0 * (acc[m : m + 128] + part)
                for p in range(2):
                    value = part[:, p * BLOCK : (p + 1) * BLOCK]
                    if added == p:
                        value = value + more[m : m + 128].astype(jnp.float32)
                    if n_out == 2:
                        outs[p][m : m + 128] = value.astype(outs[p].dtype)
                    else:
                        outs[0][p, m : m + 128] = value.astype(outs[0].dtype)


def tile(pos, row_ops, col_ops, col_at, out_dtype, n_out=1, added=None, more=()):
    depth = row_ops[0][0].shape[-2]
    rows = row_ops[0][0].shape[-1]
    plan = ([p for _, p in row_ops], [p for _, p in col_ops], col_at, depth, n_out, added)
    vmem = pl.BlockSpec(memory_space=pltpu.VMEM)
    group = SIDE * depth
    if n_out == 2:
        shapes = [jax.ShapeDtypeStruct((rows, BLOCK), out_dtype)] * 2
    else:
        shapes = jax.ShapeDtypeStruct((2, rows, BLOCK), out_dtype)
    return pl.pallas_call(
        functools.partial(tile_kernel, plan),
        out_shape=shapes,
        in_specs=[pl.BlockSpec(memory_space=pltpu.SMEM)] + [vmem] * (len(row_ops) + len(col_ops) + len(more)),
        out_specs=[vmem] * 2 if n_out == 2 else vmem,
        scratch_shapes=[
            pltpu.VMEM((group, rows), jnp.bfloat16),
            pltpu.VMEM((group, 2 * BLOCK), jnp.bfloat16),
            pltpu.VMEM((rows, 2 * BLOCK), jnp.float32),
        ],
        compiler_params=pltpu.CompilerParams(vmem_limit_bytes=16 * 2**20),
        cost_estimate=pl.CostEstimate(
            flops=1000,
            bytes_accessed=1000,
            transcendentals=0,
        ),
        name="tile",
    )(pos, *[a for a, _ in row_ops], *[a for a, _ in col_ops], *more)


def finish_kernel(first_row, pos, own, low, high, gap, *refs):
    out = refs[-1]
    rows = own.shape[1]
    row = lax.broadcasted_iota(jnp.int32, (rows, BLOCK), 0) + (2 * pos[1] + pos[3]) * WIDTH * BLOCK + first_row
    col = lax.broadcasted_iota(jnp.int32, (rows, BLOCK), 1) + (pos[0] * SIDE + pos[2]) * BLOCK
    real = own[0] + low[0].astype(jnp.float32) + high[0].astype(jnp.float32)
    out[0] = real + jnp.where(row == col, gap[...], 0.0)
    out[1] = own[1] + low[1].astype(jnp.float32) + high[1].astype(jnp.float32)


def finish(pos, first_row, own, low, high, gap, before=None):
    rows = own.shape[1]
    at = first_row // rows
    planes = pl.BlockSpec((2, rows, BLOCK), lambda i: (0, 0, 0))
    return pl.pallas_call(
        functools.partial(finish_kernel, first_row),
        grid=(1,),
        out_shape=jax.ShapeDtypeStruct((2, WIDTH * BLOCK, BLOCK), jnp.float32),
        in_specs=[pl.BlockSpec(memory_space=pltpu.SMEM)]
        + [planes] * 3
        + [pl.BlockSpec((rows, 1), lambda i: (at, 0))]
        + ([] if before is None else [pl.BlockSpec(memory_space=pl.ANY)]),
        out_specs=pl.BlockSpec((2, rows, BLOCK), lambda i: (0, at, 0)),
        input_output_aliases={} if before is None else {5: 0},
        compiler_params=pltpu.CompilerParams(vmem_limit_bytes=16 * 2**20),
        cost_estimate=pl.CostEstimate(flops=10**6, bytes_accessed=5 * 10**6, transcendentals=0),
        name="finish",
    )(pos, own, low, high, gap[:, None], *(() if before is None else (before,)))


def band_lookup(band_ids, table):
    levels = jnp.arange(table.shape[0], dtype=jnp.int32)
    onehot_mask = band_ids[:, None] == levels[None, :]
    return jnp.sum(jnp.where(onehot_mask, table[None, :], 0.0), axis=1)


def near(mine, name, axis):
    return [moved(mine, name, **{axis: step}) for step in (1, -1)]


def far(pair, name, axis, cut):
    return [moved(pair[0][:cut], name, **{axis: 1}), moved(pair[1][cut:], name, **{axis: -1})]


def swapped(held, places, name):
    return [(held, places), (moved(held, name, core=1), [(k, SIDE - 1 - zp, yp) for k, zp, yp in places])]


def row_places(mine, pair, ends):
    return [
        (mine, [(k, 0, k) for k in range(4)]),
        (pair[0], [(k, 1, k) for k in range(4)]),
        (pair[1], [(k, 2, k) for k in range(4)]),
        (ends[0], [(k, 3, k) for k in range(2)]),
        (ends[1], [(k, 3, k + 2) for k in range(2)]),
    ]


MOST = [(2 * n + k, 1 - k, n) for n in range(3) for k in range(2)]
REST = [(0, 1, 3), (1, 0, 3)]
FLIPS = (0, lambda y: 2 - lax.rem(y, 2), 3, lambda y: 1 + lax.rem(y, 2))
FLIPPED = [(2 * n + k, 1 - k, at) for n, at in enumerate(FLIPS) for k in range(2)]


def together(*groups):
    flat = lax.optimization_barrier(tuple(a for group in groups for a in group))
    result, at = [], 0
    for group in groups:
        result.append(list(flat[at : at + len(group)]))
        at += len(group)
    return result


def per_device(
    pair_density, g_index, coulomb_table, eps_valence, eps_conduction, valence_band, conduction_band
):
    wide_pos, narrow_pos = lax.axis_index("wide"), lax.axis_index("narrow")
    x, z = wide_pos // SIDE, wide_pos % SIDE
    y, c = narrow_pos // 2, narrow_pos % 2
    pos = jnp.stack([x, y, z, c]).astype(jnp.int32)

    sib = moved(pair_density, "swap", core=1)
    sib_index = moved(g_index, "swap_index", core=1)
    chip_index = jnp.where(c == 0, jnp.stack([g_index, sib_index]), jnp.stack([sib_index, g_index]))
    weight = jnp.sqrt(jnp.take(coulomb_table, chip_index.reshape(-1)))
    weight = jnp.broadcast_to(jnp.concatenate([weight, weight])[:, None], (4 * g_index.shape[0], 128))
    pieces = prepare(pos, pair_density, sib, weight)
    mine_r = pieces[:SIDE]
    cols0, cols1 = pieces[SIDE:]

    f1, f3, f2 = (moved(mine_r[k], f"r_y{k}", dy=step) for k, step in ((1, 1), (3, -1), (2, 2)))
    e0 = moved(cols0, "c_z1", per_core_z=(1, -1))
    e1 = moved(cols1, "c_z2", per_core_z=(0, 2))
    (f1, f2, f3), (e0, e1) = together((f1, f2, f3), (e0, e1))
    mine_1, mine_2 = (
        jnp.stack([a[:, CUTS[i] : CUTS[i + 1]] for a in (mine_r[0], f1, f3, f2)]) for i in range(2)
    )
    mine_a, mine_b = (jnp.stack([e0[k], e1[k]]) for k in (slice(0, 3), slice(3, 4)))

    pair_1, pair_a = together(near(mine_1, "r1_near", "dz"), near(mine_a, "ca_near", "dy"))
    most_a = swapped(jnp.concatenate([mine_a, *pair_a]), MOST, "ca_core")
    ends_1, ends_a, (most_a[1],) = together(
        far(pair_1, "r1_far", "dz", 2), far(pair_a, "ca_far", "dy", 1), (most_a[1][0],)
    )
    most_a = [most_a[0], (most_a[1], [(k, SIDE - 1 - zp, yp) for k, zp, yp in MOST])]
    cols_a = most_a + swapped(jnp.concatenate(ends_a), REST, "ca_core")
    rows_1 = row_places(mine_1, pair_1, ends_1)
    mine_2, mine_b = (after(a, *ends_1, *ends_a) for a in (mine_2, mine_b))
    pair_2 = near(mine_2, "r2_near", "dz")
    two_b = jnp.concatenate([mine_b, moved(mine_b, "cb_one", flip_y=1)])

    def first(ops, *waits):
        return [(after(ops[0][0], *waits), ops[0][1]), *ops[1:]]

    def start(rows, *waits):
        t_a = tile(pos, first(rows, *waits) if waits else rows, cols_a, 0, jnp.bfloat16, n_out=2)
        return t_a, moved(t_a[0], "x_a", dx=1), moved(t_a[1], "x_a", dx=-1)

    def send(t_b, t_c, low, high):
        t_b = jnp.stack([t_b[0] + low.astype(jnp.float32), t_b[1]]).astype(jnp.bfloat16)
        t_c = jnp.stack([t_c[0], t_c[1] + high.astype(jnp.float32)]).astype(jnp.bfloat16)
        return moved(t_b, "x_b", dx=1), moved(t_c, "x_c", dx=-1), (t_b, t_c)

    t_1a, low_1, high_1 = start(rows_1)
    pair_2, (two_b,), t_1a = together(pair_2, (two_b,), t_1a)
    more_b = moved(two_b, "cb_two", flip_y=2)
    ends_2 = far(pair_2, "r2_far", "dz", 2)
    rows_2 = row_places(mine_2, pair_2, ends_2)
    t_1b = tile(pos, first(rows_1, *t_1a, *pair_2, two_b), cols_a, 1, jnp.float32)
    t_1c = tile(pos, first(rows_1, t_1b), cols_a, 2, jnp.float32)
    x_1b, x_1c, t_1 = send(t_1b, t_1c, low_1, high_1)
    t_2a, low_2, high_2 = start(rows_2, *t_1)
    cols_b = swapped(jnp.concatenate([two_b, after(more_b, t_2a[0])]), FLIPPED, "cb_core")
    t_2b = tile(pos, first(rows_2, *t_2a), cols_a, 1, jnp.float32)
    t_2c = tile(pos, first(rows_2, t_2b), cols_a, 2, jnp.float32)
    t_2c_raw = t_2c
    t_2b, t_2c = (after(t, x_1b, x_1c) for t in (t_2b, t_2c))
    x_2b, x_2c, t_2 = send(t_2b, t_2c, low_2, high_2)
    own_1 = tile(pos, first(rows_1, t_2a[0]), cols_b, 0, jnp.float32)
    own_2 = tile(pos, first(rows_2, own_1, t_2c_raw), cols_b, 0, jnp.float32)

    gap = band_lookup(conduction_band, eps_conduction) - band_lookup(valence_band, eps_valence)
    done = finish(pos, CUTS[0], own_1, x_1b, x_1c, gap)
    return finish(pos, CUTS[1], own_2, x_2b, x_2c, gap, before=done)


def solution(mesh):
    placed = (
        P(None, ("wide", "narrow"), None),
        P(("wide", "narrow")),
        P(),
        P(),
        P(),
        P("narrow"),
        P("narrow"),
    )
    return jax.shard_map(
        per_device, mesh=mesh, in_specs=placed, out_specs=P(None, "narrow", "wide"), check_vma=False
    )
```
